32 devices in a mesh: group: 2 (over y), blk: 4 (over z), dp: 4 (over x, core).
Axes of the slice: x: 2, y: 2, z: 4, core: 2. Of those that a mesh axis runs over, the one named last changes fastest.
Arguments:
- activations: bfloat16 [1024, 4096], P(('group', 'dp'), 'blk'), parts along dimension 0, may hold values from -6 to 6
- output_grad: bfloat16 [1024, 4096], P(('group', 'dp'), 'blk'), parts along dimension 0, may hold values from -6 to 6
- gate_weight: bfloat16 [16, 128, 128, 128], P('dp', 'blk'), may hold values from -0.125 to 0.125
- up_weight: bfloat16 [16, 128, 128, 128], P('dp', 'blk'), may hold values from -0.125 to 0.125
- down_weight: bfloat16 [16, 128, 128, 128], P('dp', 'blk'), may hold values from -0.125 to 0.125
- gate_rows: int32 [112, 16], replicated, may hold values from 0 to 31, as said below
- up_rows: int32 [112, 16], replicated, may hold values from 0 to 31, as said below
- down_columns: int32 [112, 16], replicated, may hold values from 0 to 31, as said below
- owner_map: int32 [112], replicated, may hold values from 0 to 3, as said below
Outputs:
- input_grad: bfloat16 [1024, 4096], P(('group', 'dp'), 'blk'), parts along dimension 0
- gate_grad: bfloat16 [16, 256, 128, 128], P('dp', ('group', 'blk')), parts along dimension 1
- up_grad: bfloat16 [16, 256, 128, 128], P('dp', ('group', 'blk')), parts along dimension 1
- down_grad: bfloat16 [16, 256, 128, 128], P('dp', ('group', 'blk')), parts along dimension 1
The draws below stay inside these ranges and needn't reach their ends.
There are 2 independent parts, one for each index of `group`. The reference program is written for one: setup_inputs(seed, part) draws one part's arguments, and reference() takes and returns one part's arrays. A program takes and returns all parts, laid end to end along the dimension named above; an argument that names none is the same for every part. Nothing has to cross between parts.
Inputs may be any that keep to these rules, and one draw needn't show every extreme that they name: `owner_map`: each index of blk owns between 24 and 32 hidden blocks, and some index owns exactly 32. `gate_rows`: each row holds 16 distinct row blocks. `up_rows`: each row holds 16 distinct row blocks. `down_columns`: each row holds 16 distinct output blocks.
All inputs are finite; a program needn't handle non-finite values.
Results may differ from the reference program's by a relative error of at most 0.0058.
Values may be sent and summed in bfloat16 or wider, within the bound.
A program may use at most 320 MiB of HBM per device.

```python
import jax
import jax.numpy as jnp
from jax import lax

D = 4096
BS = 128
TOK_DEV = 128
DB = 32
FB = 112
KEEP = 16
HCAP = 32
SLOTS = 128
TOKENS = 512
N_BLK = 4
N_DP = 4


def kept_blocks(key):
    scores = jax.random.randint(key, (FB, DB), 0, 2 ** 20) * DB + jnp.arange(DB, dtype=jnp.int32)[None, :]
    ordering = jnp.argsort(scores, axis=1)
    return ordering[:, :KEEP].astype(jnp.int32)


def draw_gate_rows(key, part):
    key = jax.random.fold_in(key, 3)
    return kept_blocks(key)


def draw_up_rows(key, part):
    key = jax.random.fold_in(key, 5)
    return kept_blocks(key)


def draw_down_columns(key, part):
    key = jax.random.fold_in(key, 7)
    return kept_blocks(key)


def draw_owner_map(key, part):
    key = jax.random.fold_in(key, 11)
    first_key, second_key, third_key = jax.random.split(key, 3)
    average = FB // N_BLK
    surplus = HCAP - average
    pair_count = N_BLK // 2
    offsets = jax.random.randint(first_key, (pair_count,), 0, surplus + 1)
    offsets = offsets.at[0].set(surplus)
    pair_loads = jnp.stack([average + offsets, average - offsets], axis=1).reshape(N_BLK)
    placing = jax.random.permutation(second_key, N_BLK)
    loads = jnp.zeros((N_BLK,), jnp.int32).at[placing].set(pair_loads.astype(jnp.int32))
    bounds = jnp.cumsum(loads)
    indices = jnp.arange(FB, dtype=jnp.int32)
    ordered = jnp.sum((indices[:, None] >= bounds[None, :]).astype(jnp.int32), axis=1)
    shuffle = jax.random.permutation(third_key, FB)
    return ordered[shuffle].astype(jnp.int32)


def levels(own_key, shape, cuts, least, largest):
    factor_of = 1.0
    for dim, blocks in cuts:
        draws = jax.random.uniform(jax.random.fold_in(jax.random.fold_in(own_key, 6), dim), (blocks,), jnp.float32, least / len(cuts), largest / len(cuts))
        factor_of = factor_of * jnp.repeat(jnp.exp(draws), shape[dim] // blocks).reshape((-1,) + (1,) * (len(shape) - 1 - dim))
    return factor_of


def centred(stream_key, shape, scale, reach, cuts=(), kind=jnp.bfloat16):
    level = levels(stream_key, shape, cuts, -0.22, 0.18) if cuts else 1.0
    drawn = jax.random.normal(stream_key, shape, jnp.float32) * scale * level
    return jnp.minimum(jnp.maximum(drawn, -reach), reach).astype(kind)


def setup_inputs(seed: int = 0, part: int = 0) -> dict:
    keys = jax.random.split(jax.random.key(seed), 10)
    own_keys = jax.random.split(jax.random.fold_in(keys[9], part), 10)
    activations = centred(own_keys[0], (TOKENS, D), 1.0, 6.0, ((0, 4), (1, 4)))
    output_grad = centred(own_keys[1], (TOKENS, D), 1.0, 6.0, ((0, 4), (1, 4)))
    gate_weight = centred(keys[2], (KEEP, SLOTS, BS, BS), (D // 2) ** -0.5, 0.125, ((0, 4), (1, 4)))
    up_weight = centred(keys[3], (KEEP, SLOTS, BS, BS), (D // 2) ** -0.5, 0.125, ((0, 4), (1, 4)))
    down_weight = centred(keys[4], (KEEP, SLOTS, BS, BS), (D // 2) ** -0.5, 0.125, ((0, 4), (1, 4)))
    gate_rows = draw_gate_rows(jax.random.fold_in(keys[9], 71), part)
    up_rows = draw_up_rows(jax.random.fold_in(keys[9], 71), part)
    down_columns = draw_down_columns(jax.random.fold_in(keys[9], 71), part)
    owner_map = draw_owner_map(jax.random.fold_in(keys[9], 71), part)
    return {"activations": activations, "output_grad": output_grad, "gate_weight": gate_weight, "up_weight": up_weight, "down_weight": down_weight, "gate_rows": gate_rows, "up_rows": up_rows, "down_columns": down_columns, "owner_map": owner_map}


def slot_tables(owner_map):
    owners = jnp.arange(N_BLK, dtype=jnp.int32)
    owned = (owner_map[None, :] == owners[:, None]).astype(jnp.int32)
    position = jnp.cumsum(owned, axis=1) - 1
    slot_ids = jnp.arange(HCAP, dtype=jnp.int32)
    chosen = owned[:, None, :] * (position[:, None, :] == slot_ids[None, :, None]).astype(jnp.int32)
    live = jnp.sum(chosen, axis=2)
    blocks = jnp.arange(FB, dtype=jnp.int32)
    which = jnp.sum(chosen * blocks[None, None, :], axis=2)
    return live, which


def split_sum(selected, deltas, pattern):
    left = selected.reshape((N_DP, TOK_DEV) + selected.shape[1:])
    right = deltas.astype(jnp.float32).reshape((N_DP, TOK_DEV) + deltas.shape[1:])
    grouped = jnp.einsum(pattern, left, right, precision=lax.Precision.HIGHEST)
    rounded = lax.optimization_barrier(grouped.astype(jnp.bfloat16))
    return jnp.sum(rounded.astype(jnp.float32), axis=0).astype(jnp.bfloat16)


def reference(activations, output_grad, gate_weight, up_weight, down_weight, gate_rows, up_rows, down_columns, owner_map):
    live, which = slot_tables(owner_map)
    input_blocks = activations.astype(jnp.float32).reshape(TOKENS, DB, BS)
    grad_blocks = output_grad.astype(jnp.float32).reshape(TOKENS, DB, BS)

    def by_owner(weight):
        return jnp.transpose(weight.reshape(KEEP, N_BLK, HCAP, BS, BS), (1, 0, 2, 3, 4))

    owner_items = (by_owner(gate_weight), by_owner(up_weight), by_owner(down_weight),
                   gate_rows[which], up_rows[which], down_columns[which], live)
    targets = jnp.arange(DB, dtype=jnp.int32)
    highest = lax.Precision.HIGHEST

    def per_owner(running, items):
        gate_part, up_part, down_part, gate_lists, up_lists, down_lists, live_row = items
        live_mask = live_row.astype(jnp.bfloat16)[None, :, None, None]
        gate_full = (gate_part * live_mask).astype(jnp.float32)
        up_full = (up_part * live_mask).astype(jnp.float32)
        down_full = (down_part * live_mask).astype(jnp.float32)
        gate_inputs = input_blocks[:, gate_lists]
        up_inputs = input_blocks[:, up_lists]
        down_inputs = grad_blocks[:, down_lists]
        gate_value = jnp.einsum("thmc,mhcd->thd", gate_inputs, gate_full, precision=highest)
        up_value = jnp.einsum("thmc,mhcd->thd", up_inputs, up_full, precision=highest)
        backward = jnp.einsum("thme,mhce->thc", down_inputs, down_full, precision=highest)
        sigmoid_gate = jax.nn.sigmoid(gate_value)
        activated = gate_value * sigmoid_gate
        hidden = (activated * up_value).astype(jnp.bfloat16)
        up_delta = (backward * activated).astype(jnp.bfloat16)
        gate_delta = (backward * up_value * sigmoid_gate * (1.0 + gate_value * (1.0 - sigmoid_gate))).astype(jnp.bfloat16)
        gate_hits = (gate_lists[:, :, None] == targets[None, None, :]).astype(jnp.float32)
        up_hits = (up_lists[:, :, None] == targets[None, None, :]).astype(jnp.float32)
        gate_back = jnp.einsum("thd,mhcd->thmc", gate_delta.astype(jnp.float32), gate_full, precision=highest)
        up_back = jnp.einsum("thd,mhcd->thmc", up_delta.astype(jnp.float32), up_full, precision=highest)
        running = running + jnp.einsum("thmc,hmq->tqc", gate_back, gate_hits, precision=highest)
        running = running + jnp.einsum("thmc,hmq->tqc", up_back, up_hits, precision=highest)
        gate_grad = split_sum(gate_inputs, gate_delta, "nthmc,nthd->nmhcd")
        up_grad = split_sum(up_inputs, up_delta, "nthmc,nthd->nmhcd")
        down_grad = split_sum(down_inputs, hidden, "nthme,nthc->nmhce")
        return running, (gate_grad, up_grad, down_grad)

    start_sum = jnp.zeros((TOKENS, DB, BS), jnp.float32)
    total, grads = lax.scan(per_owner, start_sum, owner_items)

    def by_slot(stacked):
        return jnp.transpose(stacked, (1, 0, 2, 3, 4)).reshape(KEEP, N_BLK * HCAP, BS, BS)

    input_grad = total.reshape(TOKENS, D).astype(jnp.bfloat16)
    return (input_grad, by_slot(grads[0]), by_slot(grads[1]), by_slot(grads[2]))
```

```python
import functools

import jax
import jax.numpy as jnp
from jax import lax
from jax.experimental import pallas as pl
from jax.experimental.pallas import tpu as pltpu
from jax.sharding import PartitionSpec as P

BF16 = jnp.bfloat16
F32 = jnp.float32
CHUNKS = 4
VMEM_LIMIT = 60 * 1024 * 1024


def dot(a, b, dims):
    return lax.dot_general(a, b, (dims, ((), ())), preferred_element_type=F32)


def forward_kernel(n_dp, keep, per, offset, rows_ref, live_ref, *refs):
    token_refs = refs[:n_dp]
    gate_ref, up_ref, down_ref, out_ref = refs[n_dp:]
    slot = offset + pl.program_id(0)
    tokens = token_refs[0].shape[2]
    size = gate_ref.shape[-1]
    live = live_ref[slot]

    def picked(which, array):
        parts = []
        for m in range(keep):
            r = rows_ref[which, slot, m]
            column = pl.multiple_of(lax.rem(r, per) * size, size)
            parts.append(
                jnp.concatenate(
                    [ref[lax.div(r, per), array, :, pl.ds(column, size)] for ref in token_refs], axis=0
                )
            )
        return jnp.concatenate(parts, axis=1)

    def store(which, value):
        for i in range(n_dp):
            out_ref[i, which, 0] = value[i * tokens : (i + 1) * tokens].astype(BF16)

    @pl.when(live == 0)
    def _():
        out_ref[...] = jnp.zeros_like(out_ref)

    @pl.when(live != 0)
    def _():
        store(0, dot(picked(0, 0), gate_ref[:, 0].reshape(keep * size, size), ((1,), (0,))))
        store(1, dot(picked(1, 0), up_ref[:, 0].reshape(keep * size, size), ((1,), (0,))))
        down = jnp.concatenate([down_ref[m, 0] for m in range(keep)], axis=1)
        store(2, dot(picked(2, 1), down, ((1,), (1,))))


def backward_kernel(n_dp, keep, per, offset, first, rows_ref, *refs):
    count = 2 * n_dp + 3 + (0 if first else 4)
    inputs, (gg_ref, ug_ref, dg_ref, total_ref) = refs[:count], refs[count:]
    token_refs, delta_refs = inputs[:n_dp], inputs[n_dp : 2 * n_dp]
    turned_ref, gate_ref, up_ref = inputs[2 * n_dp : 2 * n_dp + 3]
    slot = offset + pl.program_id(0)
    tokens = token_refs[0].shape[2]
    size = gate_ref.shape[-1]

    @pl.when(pl.program_id(0) == 0)
    def _():
        if first:
            total_ref[...] = jnp.zeros_like(total_ref)
        else:
            total_ref[...] = inputs[-1][...]

    def whole(which):
        return jnp.concatenate([ref[which, 0] for ref in delta_refs], axis=0)

    for which, weight_ref, grad_ref in ((0, gate_ref, gg_ref), (1, up_ref, ug_ref)):
        delta = whole(which)
        left = jnp.concatenate([turned_ref[rows_ref[which, slot, m]] for m in range(keep)], axis=0)
        grad = dot(left, delta, ((1,), (0,))).astype(BF16)
        for m in range(keep):
            grad_ref[m, 0] = grad[m * size : (m + 1) * size]
        back = dot(delta, weight_ref[:, 0].reshape(keep * size, size), ((1,), (1,)))
        for m in range(keep):
            r = rows_ref[which, slot, m]
            column = pl.multiple_of(lax.rem(r, per) * size, size)
            for i in range(n_dp):
                at = (i, lax.div(r, per), slice(None), pl.ds(column, size))
                total_ref[at] = total_ref[at] + back[i * tokens : (i + 1) * tokens, m * size : (m + 1) * size]

    hidden = whole(2).T
    parts = []
    for m in range(keep):
        q = rows_ref[2, slot, m]
        column = pl.multiple_of(lax.rem(q, per) * size, size)
        parts.append(
            jnp.concatenate([ref[lax.div(q, per), 1, :, pl.ds(column, size)] for ref in token_refs], axis=0)
        )
    grad = dot(hidden, jnp.concatenate(parts, axis=1), ((1,), (0,))).astype(BF16)
    for m in range(keep):
        dg_ref[m, 0] = grad[:, m * size : (m + 1) * size]


def constant(shape):
    return pl.BlockSpec(shape, lambda s, *_: (0,) * len(shape), pipeline_mode=pl.Buffered(1))


def body(
    activations,
    output_grad,
    gate_weight,
    up_weight,
    down_weight,
    gate_rows,
    up_rows,
    down_columns,
    owner_map,
):
    tokens, features = activations.shape
    keep, slots, size, _ = gate_weight.shape
    n_dp, n_blk = lax.axis_size("dp"), lax.axis_size("blk")
    n_x = n_dp // 2
    per = features // size
    row_blocks = per * n_blk
    chunks = CHUNKS if slots % CHUNKS == 0 else 1
    part = slots // chunks

    def other_core(value):
        return lax.ppermute(value, "dp", [(i, i ^ 1) for i in range(n_dp)])

    def from_x(value, step):
        return lax.ppermute(value, "dp", [((i + 2 * step) % n_dp, i) for i in range(n_dp)])

    def gather_dp(value):
        column = [value] + [from_x(value, k) for k in range(1, n_x)]
        return column + [other_core(v) for v in column]

    def scatter_dp(mine, theirs):
        got = other_core(theirs)
        total = mine.astype(F32) + got.astype(F32)
        result = total[0]
        for k in range(1, n_x):
            result = result + from_x(total[k].astype(BF16), n_x - k).astype(F32)
        return result

    own = lax.axis_index("blk")
    owned = (owner_map == own).astype(jnp.int32)
    position = jnp.cumsum(owned) - 1
    slot_ids = jnp.arange(slots, dtype=jnp.int32)
    chosen = owned[None, :] * (position[None, :] == slot_ids[:, None]).astype(jnp.int32)
    live = jnp.sum(chosen, axis=1)
    listing = jnp.stack([gate_rows, up_rows, down_columns])
    listing = lax.dynamic_slice_in_dim(listing, lax.axis_index("dp") * keep, keep, axis=2)
    rows = jnp.sum(chosen[None, :, :, None] * listing[:, None, :, :], axis=2)

    both = lax.all_gather(jnp.stack([activations, output_grad]), "blk", axis=0)
    gathered = gather_dp(both)
    token_shape = (n_blk, 2, tokens, features)
    params = pltpu.CompilerParams(vmem_limit_bytes=VMEM_LIMIT)

    def weight_spec(offset):
        return pl.BlockSpec((keep, 1, size, size), lambda s, *_: (0, offset + s, 0, 0))

    flops = 6 * n_dp * tokens * part * keep * size * size
    moved = 3 * keep * part * size * size * 2 + 3 * n_dp * tokens * part * size * 2 + 8 * n_dp * tokens * row_blocks * size
    deltas = []
    for c in range(chunks):
        terms = pl.pallas_call(
            functools.partial(forward_kernel, n_dp, keep, per, c * part),
            grid_spec=pltpu.PrefetchScalarGridSpec(
                num_scalar_prefetch=2,
                grid=(part,),
                in_specs=[constant(token_shape)] * n_dp + [weight_spec(c * part)] * 3,
                out_specs=[
                    pl.BlockSpec((n_dp, 3, 1, tokens, size), lambda s, *_: (0, 0, s, 0, 0)),
                ],
            ),
            out_shape=[jax.ShapeDtypeStruct((n_dp, 3, part, tokens, size), BF16)],
            compiler_params=params,
            cost_estimate=pl.CostEstimate(flops=2 * flops, bytes_accessed=moved, transcendentals=0),
            name="forward",
        )(rows, live, *gathered, gate_weight, up_weight, down_weight)[0]
        value = scatter_dp(terms[:n_x], terms[n_x:])
        gate, up, back = value[0], value[1], value[2]
        sig = jax.nn.sigmoid(gate)
        act = gate * sig
        delta = jnp.stack(
            [
                (back * up * sig * (1.0 + gate * (1.0 - sig))).astype(BF16),
                (back * act).astype(BF16),
                (act * up).astype(BF16),
            ]
        )
        deltas.append(gather_dp(delta))

    turned = jnp.stack([g[:, 0] for g in gathered])
    turned = turned.reshape(n_dp, n_blk, tokens, per, size).transpose(1, 3, 4, 0, 2)
    turned = turned.reshape(row_blocks, size, n_dp * tokens)

    grad_shape = jax.ShapeDtypeStruct(gate_weight.shape, BF16)
    total_shape = (n_dp, n_blk, tokens, features)
    state = ()
    for c in range(chunks):
        first = c == 0
        base = 1 + 2 * n_dp + 3
        held = [] if first else [pl.BlockSpec(memory_space=pl.ANY)] * 3 + [constant(total_shape)]
        state = pl.pallas_call(
            functools.partial(backward_kernel, n_dp, keep, per, c * part, first),
            grid_spec=pltpu.PrefetchScalarGridSpec(
                num_scalar_prefetch=1,
                grid=(part,),
                in_specs=[constant(token_shape)] * n_dp
                + [pl.BlockSpec((3, 1, tokens, size), lambda s, *_: (0, s, 0, 0))] * n_dp
                + [constant((row_blocks, size, n_dp * tokens))]
                + [weight_spec(c * part)] * 2
                + held,
                out_specs=[weight_spec(c * part)] * 3 + [constant(total_shape)],
            ),
            out_shape=[grad_shape] * 3 + [jax.ShapeDtypeStruct(total_shape, F32)],
            input_output_aliases={} if first else {base + i: i for i in range(4)},
            compiler_params=params,
            cost_estimate=pl.CostEstimate(flops=3 * flops, bytes_accessed=2 * moved, transcendentals=0),
            name="backward",
        )(rows, *gathered, *deltas[c], turned, gate_weight, up_weight, *state)
    gate_grad, up_grad, down_grad, total = state

    summed = scatter_dp(total[:n_x], total[n_x:].astype(BF16))
    input_grad = lax.psum_scatter(summed, "blk", scatter_dimension=0, tiled=True)
    return input_grad.reshape(tokens, features).astype(BF16), gate_grad, up_grad, down_grad


def solution(mesh):
    in_specs = (
        P(("group", "dp"), "blk"),
        P(("group", "dp"), "blk"),
        P("dp", "blk", None, None),
        P("dp", "blk", None, None),
        P("dp", "blk", None, None),
        P(),
        P(),
        P(),
        P(),
    )
    out_specs = (
        P(("group", "dp"), "blk"),
        P("dp", ("group", "blk"), None, None),
        P("dp", ("group", "blk"), None, None),
        P("dp", ("group", "blk"), None, None),
    )
    return jax.shard_map(body, mesh=mesh, in_specs=in_specs, out_specs=out_specs, check_vma=False)
```

```python
import functools

import jax
import jax.numpy as jnp
from jax import lax
from jax.experimental import pallas as pl
from jax.experimental.pallas import tpu as pltpu
from jax.sharding import PartitionSpec as P

BF16 = jnp.bfloat16
F32 = jnp.float32
CHUNKS = 4
VMEM_LIMIT = 60 * 1024 * 1024


def dot(a, b, dims):
    return lax.dot_general(a, b, (dims, ((), ())), preferred_element_type=F32)


def picked(refs, rows_ref, which, slot, m, per, size):
    r = rows_ref[which, slot, m]
    column = pl.multiple_of(lax.rem(r, per) * size, size)
    return jnp.concatenate([ref[lax.div(r, per), :, pl.ds(column, size)] for ref in refs], axis=0)


def forward_kernel(n_dp, keep, per, offset, rows_ref, live_ref, *refs):
    token_refs, cotangent_refs = refs[:n_dp], refs[n_dp : 2 * n_dp]
    gate_ref, up_ref, down_ref, mine_ref, theirs_ref = refs[2 * n_dp :]
    slot = offset + pl.program_id(0)
    tokens = token_refs[0].shape[1]
    size = gate_ref.shape[-1]
    live = live_ref[slot]

    def side(refs, which):
        parts = [picked(refs, rows_ref, which, slot, m, per, size) for m in range(keep)]
        return jnp.concatenate(parts, axis=1)

    def store(which, value):
        for i in range(n_dp // 2):
            mine_ref[i, which, 0] = value[i * tokens : (i + 1) * tokens]
            j = n_dp // 2 + i
            theirs_ref[i, which, 0] = value[j * tokens : (j + 1) * tokens].astype(BF16)

    @pl.when(live == 0)
    def _():
        mine_ref[...] = jnp.zeros_like(mine_ref)
        theirs_ref[...] = jnp.zeros_like(theirs_ref)

    @pl.when(live != 0)
    def _():
        store(0, dot(side(token_refs, 0), gate_ref[:, 0].reshape(keep * size, size), ((1,), (0,))))
        store(1, dot(side(token_refs, 1), up_ref[:, 0].reshape(keep * size, size), ((1,), (0,))))
        down = jnp.concatenate([down_ref[m, 0] for m in range(keep)], axis=1)
        store(2, dot(side(cotangent_refs, 2), down, ((1,), (1,))))


def delta_kernel(mine_ref, got_ref, *refs):
    from_refs, out_ref = refs[:-1], refs[-1]

    def total(which):
        value = mine_ref[0, which, 0] + got_ref[0, which, 0].astype(F32)
        for ref in from_refs:
            value = value + ref[which, 0].astype(F32)
        return value

    gate, up, back = total(0), total(1), total(2)
    sig = 1.0 / (1.0 + jnp.exp(-gate))
    act = gate * sig
    out_ref[0, 0] = (back * up * sig * (1.0 + gate * (1.0 - sig))).astype(BF16)
    out_ref[1, 0] = (back * act).astype(BF16)
    out_ref[2, 0] = (act * up).astype(BF16)


def turn_kernel(*refs):
    refs, out_ref = refs[:-1], refs[-1]
    out_ref[0] = jnp.concatenate([ref[0].T for ref in refs], axis=1)


def input_kernel(n_dp, keep, per, offset, first, rows_ref, *refs):
    count = n_dp + 2 + (0 if first else 2)
    inputs, totals = refs[:count], refs[count:]
    delta_refs, (gate_ref, up_ref) = inputs[:n_dp], inputs[n_dp : n_dp + 2]
    slot = offset + pl.program_id(0)
    tokens, size = delta_refs[0].shape[2], gate_ref.shape[-1]
    n_x = n_dp // 2

    @pl.when(pl.program_id(0) == 0)
    def _():
        for i, ref in enumerate(totals):
            ref[...] = jnp.zeros_like(ref) if first else inputs[n_dp + 2 + i][...]

    for which, weight_ref in ((0, gate_ref), (1, up_ref)):
        delta = jnp.concatenate([ref[which, 0] for ref in delta_refs], axis=0)
        back = dot(delta, weight_ref[:, 0].reshape(keep * size, size), ((1,), (1,)))
        for m in range(keep):
            r = rows_ref[which, slot, m]
            column = pl.multiple_of(lax.rem(r, per) * size, size)
            for i in range(n_dp):
                ref = totals[i // n_x]
                at = (i % n_x, lax.div(r, per), slice(None), pl.ds(column, size))
                ref[at] = ref[at] + back[i * tokens : (i + 1) * tokens, m * size : (m + 1) * size]


def weight_kernel(n_dp, keep, per, offset, rows_ref, *refs):
    cotangent_refs, delta_refs = refs[:n_dp], refs[n_dp : 2 * n_dp]
    turned_ref, grads = refs[2 * n_dp], refs[-3:]
    slot = offset + pl.program_id(0)
    size = delta_refs[0].shape[-1]

    def whole(which):
        return jnp.concatenate([ref[which, 0] for ref in delta_refs], axis=0)

    for which in range(2):
        left = jnp.concatenate([turned_ref[rows_ref[which, slot, m]] for m in range(keep)], axis=0)
        grad = dot(left, whole(which), ((1,), (0,))).astype(BF16)
        for m in range(keep):
            grads[which][m, 0] = grad[m * size : (m + 1) * size]

    hidden = whole(2).T
    parts = [picked(cotangent_refs, rows_ref, 2, slot, m, per, size) for m in range(keep)]
    grad = dot(hidden, jnp.concatenate(parts, axis=1), ((1,), (0,))).astype(BF16)
    for m in range(keep):
        grads[2][m, 0] = grad[:, m * size : (m + 1) * size]


def after(rows, value):
    return rows + (value[(0,) * value.ndim] * 0).astype(jnp.int32)


def constant(shape):
    return pl.BlockSpec(shape, lambda s, *_: (0,) * len(shape), pipeline_mode=pl.Buffered(1))


def body(
    activations,
    output_grad,
    gate_weight,
    up_weight,
    down_weight,
    gate_rows,
    up_rows,
    down_columns,
    owner_map,
):
    tokens, features = activations.shape
    keep, slots, size, _ = gate_weight.shape
    n_dp, n_blk = lax.axis_size("dp"), lax.axis_size("blk")
    n_x = n_dp // 2
    per = features // size
    row_blocks = per * n_blk
    chunks = CHUNKS if slots % CHUNKS == 0 else 1
    part = slots // chunks

    def other_core(value):
        return lax.ppermute(value, "dp", [(i, i ^ 1) for i in range(n_dp)])

    def from_x(value, step):
        return lax.ppermute(value, "dp", [((i + 2 * step) % n_dp, i) for i in range(n_dp)])

    def gather_dp(value):
        column = [value] + [from_x(value, k) for k in range(1, n_x)]
        return column + [other_core(v) for v in column]

    own = lax.axis_index("blk")
    owned = (owner_map == own).astype(jnp.int32)
    position = jnp.cumsum(owned) - 1
    slot_ids = jnp.arange(slots, dtype=jnp.int32)
    chosen = owned[None, :] * (position[None, :] == slot_ids[:, None]).astype(jnp.int32)
    live = jnp.sum(chosen, axis=1)
    listing = jnp.stack([gate_rows, up_rows, down_columns])
    listing = lax.dynamic_slice_in_dim(listing, lax.axis_index("dp") * keep, keep, axis=2)
    rows = jnp.sum(chosen[None, :, :, None] * listing[:, None, :, :], axis=2)

    inputs = gather_dp(lax.all_gather(activations, "blk", axis=0))
    cotangents = gather_dp(lax.all_gather(output_grad, "blk", axis=0))
    token_shape = (n_blk, tokens, features)
    params = pltpu.CompilerParams(vmem_limit_bytes=VMEM_LIMIT)

    def weight_spec(offset):
        return pl.BlockSpec((keep, 1, size, size), lambda s, *_: (0, offset + s, 0, 0))

    per_slot = pl.BlockSpec((3, 1, tokens, size), lambda s, *_: (0, s, 0, 0))
    per_column = pl.BlockSpec((n_x, 3, 1, tokens, size), lambda s, *_: (0, 0, s, 0, 0))
    column_shape = (n_x, 3, part, tokens, size)
    delta_shape = jax.ShapeDtypeStruct((3, part, tokens, size), BF16)

    halves, sends = [], []
    for c in range(chunks):
        order = after(rows, sends[c - 2]) if c >= 2 else rows
        mine, theirs = pl.pallas_call(
            functools.partial(forward_kernel, n_dp, keep, per, c * part),
            grid_spec=pltpu.PrefetchScalarGridSpec(
                num_scalar_prefetch=2,
                grid=(part,),
                in_specs=[constant(token_shape)] * (2 * n_dp) + [weight_spec(c * part)] * 3,
                out_specs=[per_column] * 2,
            ),
            out_shape=[jax.ShapeDtypeStruct(column_shape, F32), jax.ShapeDtypeStruct(column_shape, BF16)],
            compiler_params=params,
            name="forward",
        )(order, live, *inputs, *cotangents, gate_weight, up_weight, down_weight)
        got = other_core(theirs)
        send = (mine[1:] + got[1:].astype(F32)).astype(BF16)
        sends.append(send)
        halves.append((mine, got, [from_x(send[k - 1], n_x - k) for k in range(1, n_x)]))

    turned = pl.pallas_call(
        turn_kernel,
        grid=(row_blocks,),
        in_specs=[pl.BlockSpec((1, tokens, size), lambda r: (r // per, 0, r % per))] * n_dp,
        out_specs=pl.BlockSpec((1, size, n_dp * tokens), lambda r: (r, 0, 0)),
        out_shape=jax.ShapeDtypeStruct((row_blocks, size, n_dp * tokens), BF16),
        name="turn",
    )(*inputs)

    deltas = []
    for mine, got, arrived in halves:
        delta = pl.pallas_call(
            delta_kernel,
            grid=(part,),
            in_specs=[pl.BlockSpec((1, 3, 1, tokens, size), lambda s: (0, 0, s, 0, 0))] * 2 + [per_slot] * (n_x - 1),
            out_specs=per_slot,
            out_shape=delta_shape,
            name="delta",
        )(mine, got, *arrived)
        deltas.append(gather_dp(delta))

    total_shape = (n_x, n_blk, tokens, features)
    totals = ()
    for c in range(chunks):
        first = c == 0
        held = [constant(total_shape)] * len(totals)
        totals = pl.pallas_call(
            functools.partial(input_kernel, n_dp, keep, per, c * part, first),
            grid_spec=pltpu.PrefetchScalarGridSpec(
                num_scalar_prefetch=1,
                grid=(part,),
                in_specs=[per_slot] * n_dp + [weight_spec(c * part)] * 2 + held,
                out_specs=[constant(total_shape)] * 2,
            ),
            out_shape=[jax.ShapeDtypeStruct(total_shape, F32)] * 2,
            input_output_aliases={} if first else {n_dp + 3 + i: i for i in range(2)},
            compiler_params=params,
            name="input",
        )(rows, *deltas[c], gate_weight, up_weight, *totals)

    mine, theirs = totals[0], totals[1].astype(BF16)
    got = other_core(theirs)
    send = (mine[1:] + got[1:].astype(F32)).astype(BF16)
    summed = mine[0] + got[0].astype(F32)
    for k in range(1, n_x):
        summed = summed + from_x(send[k - 1], n_x - k).astype(F32)
    rounded = summed.astype(BF16)

    def for_blk(array, step):
        return lax.dynamic_index_in_dim(array, lax.rem(own + step, n_blk), 0, keepdims=False)

    pieces = [
        lax.ppermute(for_blk(rounded, k), "blk", [(i, (i + k) % n_blk) for i in range(n_blk)])
        for k in range(1, n_blk)
    ]
    input_grad = for_blk(summed, 0)
    for piece in pieces:
        input_grad = input_grad + piece.astype(F32)

    grads = ()
    grad_shape = jax.ShapeDtypeStruct(gate_weight.shape, BF16)
    for c in range(chunks):
        order = rows
        if c == chunks - 1:
            order = after(rows, rounded)
        elif c > 0:
            order = after(rows, send if c >= 2 else theirs)
        held = [pl.BlockSpec(memory_space=pl.ANY)] * len(grads)
        grads = pl.pallas_call(
            functools.partial(weight_kernel, n_dp, keep, per, c * part),
            grid_spec=pltpu.PrefetchScalarGridSpec(
                num_scalar_prefetch=1,
                grid=(part,),
                in_specs=[constant(token_shape)] * n_dp
                + [per_slot] * n_dp
                + [constant((row_blocks, size, n_dp * tokens))]
                + held,
                out_specs=[weight_spec(c * part)] * 3,
            ),
            out_shape=[grad_shape] * 3,
            input_output_aliases={2 * n_dp + 2 + i: i for i in range(len(grads))},
            compiler_params=params,
            name="weight",
        )(order, *cotangents, *deltas[c], turned, *grads)
    return input_grad.astype(BF16), *grads


def solution(mesh):
    in_specs = (
        P(("group", "dp"), "blk"),
        P(("group", "dp"), "blk"),
        P("dp", "blk", None, None),
        P("dp", "blk", None, None),
        P("dp", "blk", None, None),
        P(),
        P(),
        P(),
        P(),
    )
    out_specs = (
        P(("group", "dp"), "blk"),
        P("dp", ("group", "blk"), None, None),
        P("dp", ("group", "blk"), None, None),
        P("dp", ("group", "blk"), None, None),
    )
    return jax.shard_map(body, mesh=mesh, in_specs=in_specs, out_specs=out_specs, check_vma=False)
```

```python
import functools

import jax
import jax.numpy as jnp
from jax import lax
from jax.experimental import pallas as pl
from jax.experimental.pallas import tpu as pltpu
from jax.sharding import PartitionSpec as P

BF16 = jnp.bfloat16
F32 = jnp.float32
CHUNKS = 4
VMEM_LIMIT = 60 * 1024 * 1024
LITTLE = pl.CostEstimate(flops=1, bytes_accessed=1, transcendentals=0)


def dot(a, b, dims):
    return lax.dot_general(a, b, (dims, ((), ())), preferred_element_type=F32)


def picked(refs, rows_ref, which, slot, m, per, size):
    r = rows_ref[which, slot, m]
    column = pl.multiple_of(lax.rem(r, per) * size, size)
    return jnp.concatenate([ref[lax.div(r, per), :, pl.ds(column, size)] for ref in refs], axis=0)


def forward_kernel(n_dp, keep, per, offset, rows_ref, live_ref, *refs):
    token_refs, cotangent_refs = refs[:n_dp], refs[n_dp : 2 * n_dp]
    gate_ref, up_ref, down_ref, mine_ref, theirs_ref = refs[2 * n_dp :]
    slot = offset + pl.program_id(0)
    tokens = token_refs[0].shape[1]
    size = gate_ref.shape[-1]
    live = live_ref[slot]

    def side(refs, which):
        parts = [picked(refs, rows_ref, which, slot, m, per, size) for m in range(keep)]
        return jnp.concatenate(parts, axis=1)

    def store(which, value):
        for i in range(n_dp // 2):
            mine_ref[i, which, 0] = value[i * tokens : (i + 1) * tokens]
            j = n_dp // 2 + i
            theirs_ref[i, which, 0] = value[j * tokens : (j + 1) * tokens].astype(BF16)

    @pl.when(live == 0)
    def _():
        mine_ref[...] = jnp.zeros_like(mine_ref)
        theirs_ref[...] = jnp.zeros_like(theirs_ref)

    @pl.when(live != 0)
    def _():
        store(0, dot(side(token_refs, 0), gate_ref[:, 0].reshape(keep * size, size), ((1,), (0,))))
        store(1, dot(side(token_refs, 1), up_ref[:, 0].reshape(keep * size, size), ((1,), (0,))))
        down = jnp.concatenate([down_ref[m, 0] for m in range(keep)], axis=1)
        store(2, dot(side(cotangent_refs, 2), down, ((1,), (1,))))


def delta_kernel(mine_ref, got_ref, *refs):
    from_refs, out_ref = refs[:-1], refs[-1]

    def total(which):
        value = mine_ref[0, which, 0] + got_ref[0, which, 0].astype(F32)
        for ref in from_refs:
            value = value + ref[which, 0].astype(F32)
        return value

    gate, up, back = total(0), total(1), total(2)
    sig = 1.0 / (1.0 + jnp.exp(-gate))
    act = gate * sig
    out_ref[0, 0] = (back * up * sig * (1.0 + gate * (1.0 - sig))).astype(BF16)
    out_ref[1, 0] = (back * act).astype(BF16)
    out_ref[2, 0] = (act * up).astype(BF16)


def turn_kernel(*refs):
    refs, out_ref = refs[:-1], refs[-1]
    out_ref[0] = jnp.concatenate([ref[0].T for ref in refs], axis=1)


def input_kernel(n_dp, keep, per, offset, first, rows_ref, *refs):
    count = n_dp + 2 + (0 if first else 2)
    inputs, totals = refs[:count], refs[count:]
    delta_refs, (gate_ref, up_ref) = inputs[:n_dp], inputs[n_dp : n_dp + 2]
    slot = offset + pl.program_id(0)
    tokens, size = delta_refs[0].shape[2], gate_ref.shape[-1]
    n_x = n_dp // 2

    @pl.when(pl.program_id(0) == 0)
    def _():
        for i, ref in enumerate(totals):
            ref[...] = jnp.zeros_like(ref) if first else inputs[n_dp + 2 + i][...]

    for which, weight_ref in ((0, gate_ref), (1, up_ref)):
        delta = jnp.concatenate([ref[which, 0] for ref in delta_refs], axis=0)
        back = dot(delta, weight_ref[:, 0].reshape(keep * size, size), ((1,), (1,)))
        for m in range(keep):
            r = rows_ref[which, slot, m]
            column = pl.multiple_of(lax.rem(r, per) * size, size)
            for i in range(n_dp):
                ref = totals[i // n_x]
                at = (i % n_x, lax.div(r, per), slice(None), pl.ds(column, size))
                ref[at] = ref[at] + back[i * tokens : (i + 1) * tokens, m * size : (m + 1) * size]


def weight_kernel(n_dp, keep, per, offset, rows_ref, *refs):
    cotangent_refs, delta_refs = refs[:n_dp], refs[n_dp : 2 * n_dp]
    turned_ref, grads = refs[2 * n_dp], refs[-3:]
    slot = offset + pl.program_id(0)
    size = delta_refs[0].shape[-1]

    def whole(which):
        return jnp.concatenate([ref[which, 0] for ref in delta_refs], axis=0)

    for which in range(2):
        left = jnp.concatenate([turned_ref[rows_ref[which, slot, m]] for m in range(keep)], axis=0)
        grad = dot(left, whole(which), ((1,), (0,))).astype(BF16)
        for m in range(keep):
            grads[which][m, 0] = grad[m * size : (m + 1) * size]

    hidden = whole(2).T
    parts = [picked(cotangent_refs, rows_ref, 2, slot, m, per, size) for m in range(keep)]
    grad = dot(hidden, jnp.concatenate(parts, axis=1), ((1,), (0,))).astype(BF16)
    for m in range(keep):
        grads[2][m, 0] = grad[:, m * size : (m + 1) * size]


def after(array, *values):
    for value in values:
        array = array + (value[(0,) * value.ndim] * 0).astype(array.dtype)
    return array


def constant(shape):
    return pl.BlockSpec(shape, lambda s, *_: (0,) * len(shape), pipeline_mode=pl.Buffered(1))


def body(
    activations,
    output_grad,
    gate_weight,
    up_weight,
    down_weight,
    gate_rows,
    up_rows,
    down_columns,
    owner_map,
):
    tokens, features = activations.shape
    keep, slots, size, _ = gate_weight.shape
    n_dp, n_blk = lax.axis_size("dp"), lax.axis_size("blk")
    n_x = n_dp // 2
    per = features // size
    row_blocks = per * n_blk
    chunks = CHUNKS if slots % CHUNKS == 0 else 1
    part = slots // chunks

    def other_core(value):
        return lax.ppermute(value, "dp", [(i, i ^ 1) for i in range(n_dp)])

    def from_x(value, step):
        return lax.ppermute(value, "dp", [((i + 2 * step) % n_dp, i) for i in range(n_dp)])

    def gather_dp(value):
        column = [value] + [from_x(value, k) for k in range(1, n_x)]
        return column + [other_core(v) for v in column]

    own = lax.axis_index("blk")
    owned = (owner_map == own).astype(jnp.int32)
    position = jnp.cumsum(owned) - 1
    slot_ids = jnp.arange(slots, dtype=jnp.int32)
    chosen = owned[None, :] * (position[None, :] == slot_ids[:, None]).astype(jnp.int32)
    live = jnp.sum(chosen, axis=1)
    listing = jnp.stack([gate_rows, up_rows, down_columns])
    listing = lax.dynamic_slice_in_dim(listing, lax.axis_index("dp") * keep, keep, axis=2)
    rows = jnp.sum(chosen[None, :, :, None] * listing[:, None, :, :], axis=2)

    inputs = gather_dp(lax.all_gather(activations, "blk", axis=0))
    cotangents = gather_dp(lax.all_gather(output_grad, "blk", axis=0))
    token_shape = (n_blk, tokens, features)
    params = pltpu.CompilerParams(vmem_limit_bytes=VMEM_LIMIT)

    def weight_spec(offset):
        return pl.BlockSpec((keep, 1, size, size), lambda s, *_: (0, offset + s, 0, 0))

    per_slot = pl.BlockSpec((3, 1, tokens, size), lambda s, *_: (0, s, 0, 0))
    per_column = pl.BlockSpec((n_x, 3, 1, tokens, size), lambda s, *_: (0, 0, s, 0, 0))
    column_shape = (n_x, 3, part, tokens, size)
    delta_shape = jax.ShapeDtypeStruct((3, part, tokens, size), BF16)

    turned = pl.pallas_call(
        turn_kernel,
        grid=(row_blocks,),
        in_specs=[pl.BlockSpec((1, tokens, size), lambda r: (r // per, 0, r % per))] * n_dp,
        out_specs=pl.BlockSpec((1, size, n_dp * tokens), lambda r: (r, 0, 0)),
        out_shape=jax.ShapeDtypeStruct((row_blocks, size, n_dp * tokens), BF16),
        cost_estimate=LITTLE,
        name="turn",
    )(*inputs)

    def forward(c, order):
        mine, theirs = pl.pallas_call(
            functools.partial(forward_kernel, n_dp, keep, per, c * part),
            grid_spec=pltpu.PrefetchScalarGridSpec(
                num_scalar_prefetch=2,
                grid=(part,),
                in_specs=[constant(token_shape)] * (2 * n_dp) + [weight_spec(c * part)] * 3,
                out_specs=[per_column] * 2,
            ),
            out_shape=[jax.ShapeDtypeStruct(column_shape, F32), jax.ShapeDtypeStruct(column_shape, BF16)],
            compiler_params=params,
            cost_estimate=LITTLE,
            name="forward",
        )(order, live, *inputs, *cotangents, gate_weight, up_weight, down_weight)
        return mine, other_core(theirs)

    def to_delta(mine, got, arrived):
        return pl.pallas_call(
            delta_kernel,
            grid=(part,),
            in_specs=[pl.BlockSpec((1, 3, 1, tokens, size), lambda s: (0, 0, s, 0, 0))] * 2 + [per_slot] * (n_x - 1),
            out_specs=per_slot,
            out_shape=delta_shape,
            cost_estimate=LITTLE,
            name="delta",
        )(mine, got, *arrived)

    sends, own_deltas, columns = [], [], []
    for c in range(chunks):
        if c == 0:
            order = after(rows, turned)
        elif c == 1:
            order = rows
        elif c == 2:
            order = after(rows, sends[0])
        else:
            order = after(rows, own_deltas[c - 3])
        mine, got = forward(c, order)
        send = mine[1:] + got[1:].astype(F32)
        if c >= 2:
            send = after(send, own_deltas[c - 2])
        send = send.astype(BF16)
        sends.append(send)
        delta = to_delta(mine, got, [from_x(send[k - 1], n_x - k) for k in range(1, n_x)])
        own_deltas.append(delta)
        columns.append([from_x(delta, k) for k in range(1, n_x)])

    grad_shape = jax.ShapeDtypeStruct(gate_weight.shape, BF16)

    def weights(c, order, grads):
        return pl.pallas_call(
            functools.partial(weight_kernel, n_dp, keep, per, c * part),
            grid_spec=pltpu.PrefetchScalarGridSpec(
                num_scalar_prefetch=1,
                grid=(part,),
                in_specs=[constant(token_shape)] * n_dp
                + [per_slot] * n_dp
                + [constant((row_blocks, size, n_dp * tokens))]
                + [pl.BlockSpec(memory_space=pl.ANY)] * len(grads),
                out_specs=[weight_spec(c * part)] * 3,
            ),
            out_shape=[grad_shape] * 3,
            input_output_aliases={2 * n_dp + 2 + i: i for i in range(len(grads))},
            compiler_params=params,
            cost_estimate=LITTLE,
            name="weight",
        )(order, *cotangents, *deltas[c], turned, *grads)

    total_shape = (n_x, n_blk, tokens, features)
    totals, grads, deltas = (), (), []
    for c in range(chunks):
        first = c == 0
        column = columns[c]
        if not first:
            ready = [totals[0]] + ([own_deltas[c + 1]] if c + 1 < chunks else [])
            column = [after(v, *ready) for v in column]
        column = [own_deltas[c]] + columns[c], [other_core(own_deltas[c])] + [other_core(v) for v in column]
        deltas.append(column[0] + column[1])
        order = after(rows, grads[0]) if c == 1 else rows
        held = [constant(total_shape)] * len(totals)
        totals = pl.pallas_call(
            functools.partial(input_kernel, n_dp, keep, per, c * part, first),
            grid_spec=pltpu.PrefetchScalarGridSpec(
                num_scalar_prefetch=1,
                grid=(part,),
                in_specs=[per_slot] * n_dp + [weight_spec(c * part)] * 2 + held,
                out_specs=[constant(total_shape)] * 2,
            ),
            out_shape=[jax.ShapeDtypeStruct(total_shape, F32)] * 2,
            input_output_aliases={} if first else {n_dp + 3 + i: i for i in range(2)},
            compiler_params=params,
            cost_estimate=LITTLE,
            name="input",
        )(order, *deltas[c], gate_weight, up_weight, *totals)
        if first:
            grads = weights(0, rows, grads)

    mine, theirs = totals[0], totals[1].astype(BF16)
    got = other_core(theirs)
    send = (mine[1:] + got[1:].astype(F32)).astype(BF16)
    summed = mine[0] + got[0].astype(F32)
    for k in range(1, n_x):
        summed = summed + from_x(send[k - 1], n_x - k).astype(F32)
    for c in range(1, chunks - 1):
        grads = weights(c, after(rows, send), grads)
    summed = after(summed, grads[0])
    rounded = summed.astype(BF16)
    if chunks > 1:
        grads = weights(chunks - 1, after(rows, rounded), grads)

    def for_blk(array, step):
        return lax.dynamic_index_in_dim(array, lax.rem(own + step, n_blk), 0, keepdims=False)

    pieces = [
        lax.ppermute(for_blk(rounded, k), "blk", [(i, (i + k) % n_blk) for i in range(n_blk)])
        for k in range(1, n_blk)
    ]
    input_grad = for_blk(summed, 0)
    for piece in pieces:
        input_grad = input_grad + piece.astype(F32)

    return input_grad.astype(BF16), *grads


def solution(mesh):
    in_specs = (
        P(("group", "dp"), "blk"),
        P(("group", "dp"), "blk"),
        P("dp", "blk", None, None),
        P("dp", "blk", None, None),
        P("dp", "blk", None, None),
        P(),
        P(),
        P(),
        P(),
    )
    out_specs = (
        P(("group", "dp"), "blk"),
        P("dp", ("group", "blk"), None, None),
        P("dp", ("group", "blk"), None, None),
        P("dp", ("group", "blk"), None, None),
    )
    return jax.shard_map(body, mesh=mesh, in_specs=in_specs, out_specs=out_specs, check_vma=False)
```

```python
import functools

import jax
import jax.numpy as jnp
from jax import lax
from jax.experimental import pallas as pl
from jax.experimental.pallas import tpu as pltpu
from jax.sharding import PartitionSpec as P

BF16 = jnp.bfloat16
F32 = jnp.float32
CHUNKS = 4
VMEM_LIMIT = 60 * 1024 * 1024
LITTLE = pl.CostEstimate(flops=1, bytes_accessed=1, transcendentals=0)


def dot(a, b, dims):
    return lax.dot_general(a, b, (dims, ((), ())), preferred_element_type=F32)


def picked(refs, rows_ref, which, slot, m, per, size):
    r = rows_ref[which, slot, m]
    column = pl.multiple_of(lax.rem(r, per) * size, size)
    return jnp.concatenate([ref[lax.div(r, per), :, pl.ds(column, size)] for ref in refs], axis=0)


def forward_kernel(n_dp, keep, per, offset, rows_ref, live_ref, *refs):
    token_refs, cotangent_refs = refs[:n_dp], refs[n_dp : 2 * n_dp]
    gate_ref, up_ref, down_ref, mine_ref, theirs_ref = refs[2 * n_dp :]
    slot = offset + pl.program_id(0)
    tokens = token_refs[0].shape[1]
    size = gate_ref.shape[-1]
    live = live_ref[slot]

    def side(refs, which):
        parts = [picked(refs, rows_ref, which, slot, m, per, size) for m in range(keep)]
        return jnp.concatenate(parts, axis=1)

    def store(which, value):
        for i in range(n_dp // 2):
            mine_ref[i, which, 0] = value[i * tokens : (i + 1) * tokens]
            j = n_dp // 2 + i
            theirs_ref[i, which, 0] = value[j * tokens : (j + 1) * tokens].astype(BF16)

    @pl.when(live == 0)
    def _():
        mine_ref[...] = jnp.zeros_like(mine_ref)
        theirs_ref[...] = jnp.zeros_like(theirs_ref)

    @pl.when(live != 0)
    def _():
        store(0, dot(side(token_refs, 0), gate_ref[:, 0].reshape(keep * size, size), ((1,), (0,))))
        store(1, dot(side(token_refs, 1), up_ref[:, 0].reshape(keep * size, size), ((1,), (0,))))
        down = jnp.concatenate([down_ref[m, 0] for m in range(keep)], axis=1)
        store(2, dot(side(cotangent_refs, 2), down, ((1,), (1,))))


def delta_kernel(mine_ref, got_ref, *refs):
    from_refs, out_ref = refs[:-1], refs[-1]

    def total(which):
        value = mine_ref[0, which, 0] + got_ref[0, which, 0].astype(F32)
        for ref in from_refs:
            value = value + ref[which, 0].astype(F32)
        return value

    gate, up, back = total(0), total(1), total(2)
    sig = 1.0 / (1.0 + jnp.exp(-gate))
    act = gate * sig
    out_ref[0, 0] = (back * up * sig * (1.0 + gate * (1.0 - sig))).astype(BF16)
    out_ref[1, 0] = (back * act).astype(BF16)
    out_ref[2, 0] = (act * up).astype(BF16)


def turn_kernel(*refs):
    refs, out_ref = refs[:-1], refs[-1]
    out_ref[0] = jnp.concatenate([ref[0].T for ref in refs], axis=1)


def input_kernel(n_dp, keep, per, offset, first, rows_ref, *refs):
    count = n_dp + 2 + (0 if first else 2)
    inputs, totals = refs[:count], refs[count:]
    delta_refs, (gate_ref, up_ref) = inputs[:n_dp], inputs[n_dp : n_dp + 2]
    slot = offset + pl.program_id(0)
    tokens, size = delta_refs[0].shape[2], gate_ref.shape[-1]
    n_x = n_dp // 2

    @pl.when(pl.program_id(0) == 0)
    def _():
        for i, ref in enumerate(totals):
            ref[...] = jnp.zeros_like(ref) if first else inputs[n_dp + 2 + i][...]

    for which, weight_ref in ((0, gate_ref), (1, up_ref)):
        delta = jnp.concatenate([ref[which, 0] for ref in delta_refs], axis=0)
        back = dot(delta, weight_ref[:, 0].reshape(keep * size, size), ((1,), (1,)))
        for m in range(keep):
            r = rows_ref[which, slot, m]
            column = pl.multiple_of(lax.rem(r, per) * size, size)
            for i in range(n_dp):
                ref = totals[i // n_x]
                at = (i % n_x, lax.div(r, per), slice(None), pl.ds(column, size))
                ref[at] = ref[at] + back[i * tokens : (i + 1) * tokens, m * size : (m + 1) * size]


def weight_kernel(n_dp, keep, per, offset, rows_ref, *refs):
    cotangent_refs, delta_refs = refs[:n_dp], refs[n_dp : 2 * n_dp]
    turned_ref, grads = refs[2 * n_dp], refs[-3:]
    slot = offset + pl.program_id(0)
    size = delta_refs[0].shape[-1]

    def whole(which):
        return jnp.concatenate([ref[which, 0] for ref in delta_refs], axis=0)

    for which in range(2):
        left = jnp.concatenate([turned_ref[rows_ref[which, slot, m]] for m in range(keep)], axis=0)
        grad = dot(left, whole(which), ((1,), (0,))).astype(BF16)
        for m in range(keep):
            grads[which][m, 0] = grad[m * size : (m + 1) * size]

    hidden = whole(2).T
    parts = [picked(cotangent_refs, rows_ref, 2, slot, m, per, size) for m in range(keep)]
    grad = dot(hidden, jnp.concatenate(parts, axis=1), ((1,), (0,))).astype(BF16)
    for m in range(keep):
        grads[2][m, 0] = grad[:, m * size : (m + 1) * size]


def after(array, *values):
    for value in values:
        array = array + (value[(0,) * value.ndim] * 0).astype(array.dtype)
    return array


def constant(shape):
    return pl.BlockSpec(shape, lambda s, *_: (0,) * len(shape), pipeline_mode=pl.Buffered(1))


def body(
    activations,
    output_grad,
    gate_weight,
    up_weight,
    down_weight,
    gate_rows,
    up_rows,
    down_columns,
    owner_map,
):
    tokens, features = activations.shape
    keep, slots, size, _ = gate_weight.shape
    n_dp, n_blk = lax.axis_size("dp"), lax.axis_size("blk")
    n_x = n_dp // 2
    per = features // size
    row_blocks = per * n_blk
    chunks = CHUNKS if slots % CHUNKS == 0 else 1
    part = slots // chunks

    def other_core(value):
        return lax.ppermute(value, "dp", [(i, i ^ 1) for i in range(n_dp)])

    def from_x(value, step):
        return lax.ppermute(value, "dp", [((i + 2 * step) % n_dp, i) for i in range(n_dp)])

    def gather_dp(value):
        column = [value] + [from_x(value, k) for k in range(1, n_x)]
        return column + [other_core(v) for v in column]

    own = lax.axis_index("blk")
    owned = (owner_map == own).astype(jnp.int32)
    position = jnp.cumsum(owned) - 1
    slot_ids = jnp.arange(slots, dtype=jnp.int32)
    chosen = owned[None, :] * (position[None, :] == slot_ids[:, None]).astype(jnp.int32)
    live = jnp.sum(chosen, axis=1)
    listing = jnp.stack([gate_rows, up_rows, down_columns])
    listing = lax.dynamic_slice_in_dim(listing, lax.axis_index("dp") * keep, keep, axis=2)
    rows = jnp.sum(chosen[None, :, :, None] * listing[:, None, :, :], axis=2)

    inputs = gather_dp(lax.all_gather(activations, "blk", axis=0))
    cotangents = lax.all_gather(output_grad, "blk", axis=0)
    cotangents = [cotangents] + [from_x(cotangents, k) for k in range(1, n_x)]
    token_shape = (n_blk, tokens, features)
    params = pltpu.CompilerParams(vmem_limit_bytes=VMEM_LIMIT)

    def weight_spec(offset):
        return pl.BlockSpec((keep, 1, size, size), lambda s, *_: (0, offset + s, 0, 0))

    per_slot = pl.BlockSpec((3, 1, tokens, size), lambda s, *_: (0, s, 0, 0))
    per_column = pl.BlockSpec((n_x, 3, 1, tokens, size), lambda s, *_: (0, 0, s, 0, 0))
    column_shape = (n_x, 3, part, tokens, size)
    delta_shape = jax.ShapeDtypeStruct((3, part, tokens, size), BF16)

    turned = pl.pallas_call(
        turn_kernel,
        grid=(row_blocks,),
        in_specs=[pl.BlockSpec((1, tokens, size), lambda r: (r // per, 0, r % per))] * n_dp,
        out_specs=pl.BlockSpec((1, size, n_dp * tokens), lambda r: (r, 0, 0)),
        out_shape=jax.ShapeDtypeStruct((row_blocks, size, n_dp * tokens), BF16),
        cost_estimate=LITTLE,
        name="turn",
    )(*inputs)
    cotangents = cotangents + [other_core(cotangents[0])] + [other_core(after(v, turned)) for v in cotangents[1:]]

    def forward(c, order):
        mine, theirs = pl.pallas_call(
            functools.partial(forward_kernel, n_dp, keep, per, c * part),
            grid_spec=pltpu.PrefetchScalarGridSpec(
                num_scalar_prefetch=2,
                grid=(part,),
                in_specs=[constant(token_shape)] * (2 * n_dp) + [weight_spec(c * part)] * 3,
                out_specs=[per_column] * 2,
            ),
            out_shape=[jax.ShapeDtypeStruct(column_shape, F32), jax.ShapeDtypeStruct(column_shape, BF16)],
            compiler_params=params,
            cost_estimate=LITTLE,
            name="forward",
        )(order, live, *inputs, *cotangents, gate_weight, up_weight, down_weight)
        return mine, other_core(theirs)

    def to_delta(mine, got, arrived):
        return pl.pallas_call(
            delta_kernel,
            grid=(part,),
            in_specs=[pl.BlockSpec((1, 3, 1, tokens, size), lambda s: (0, 0, s, 0, 0))] * 2 + [per_slot] * (n_x - 1),
            out_specs=per_slot,
            out_shape=delta_shape,
            cost_estimate=LITTLE,
            name="delta",
        )(mine, got, *arrived)

    sends, own_deltas, columns, halves = [], [], [], []

    def finish(c, *values):
        mine, got, arrived = halves[c]
        delta = to_delta(mine, got, [after(v, *values) for v in arrived])
        own_deltas.append(delta)
        columns.append([from_x(delta, k) for k in range(1, n_x)])

    for c in range(chunks):
        if c == 0:
            order = after(rows, turned)
        elif c == 2:
            order = after(rows, own_deltas[0])
        else:
            order = after(rows, sends[c - 1])
        mine, got = forward(c, order)
        if c == 1:
            finish(0, mine)
        elif c == 2:
            finish(1, mine)
        send = mine[1:] + got[1:].astype(F32)
        if c >= 2:
            send = after(send, own_deltas[c - 2])
        send = send.astype(BF16)
        sends.append(send)
        halves.append((mine, got, [from_x(send[k - 1], n_x - k) for k in range(1, n_x)]))
    for c in range(len(own_deltas), chunks):
        finish(c)

    grad_shape = jax.ShapeDtypeStruct(gate_weight.shape, BF16)

    def weights(c, order, grads):
        return pl.pallas_call(
            functools.partial(weight_kernel, n_dp, keep, per, c * part),
            grid_spec=pltpu.PrefetchScalarGridSpec(
                num_scalar_prefetch=1,
                grid=(part,),
                in_specs=[constant(token_shape)] * n_dp
                + [per_slot] * n_dp
                + [constant((row_blocks, size, n_dp * tokens))]
                + [pl.BlockSpec(memory_space=pl.ANY)] * len(grads),
                out_specs=[weight_spec(c * part)] * 3,
            ),
            out_shape=[grad_shape] * 3,
            input_output_aliases={2 * n_dp + 2 + i: i for i in range(len(grads))},
            compiler_params=params,
            cost_estimate=LITTLE,
            name="weight",
        )(order, *cotangents, *deltas[c], turned, *grads)

    total_shape = (n_x, n_blk, tokens, features)
    totals, grads, deltas = (), (), []
    for c in range(chunks):
        first = c == 0
        column = columns[c]
        if not first:
            ready = [totals[0]] + ([own_deltas[c + 1]] if c + 1 < chunks else [])
            column = [after(v, *ready) for v in column]
        column = [own_deltas[c]] + columns[c], [other_core(own_deltas[c])] + [other_core(v) for v in column]
        deltas.append(column[0] + column[1])
        order = after(rows, grads[0]) if c == 1 else rows
        held = [constant(total_shape)] * len(totals)
        totals = pl.pallas_call(
            functools.partial(input_kernel, n_dp, keep, per, c * part, first),
            grid_spec=pltpu.PrefetchScalarGridSpec(
                num_scalar_prefetch=1,
                grid=(part,),
                in_specs=[per_slot] * n_dp + [weight_spec(c * part)] * 2 + held,
                out_specs=[constant(total_shape)] * 2,
            ),
            out_shape=[jax.ShapeDtypeStruct(total_shape, F32)] * 2,
            input_output_aliases={} if first else {n_dp + 3 + i: i for i in range(2)},
            compiler_params=params,
            cost_estimate=LITTLE,
            name="input",
        )(order, *deltas[c], gate_weight, up_weight, *totals)
        if first:
            grads = weights(0, rows, grads)

    mine, theirs = totals[0], totals[1].astype(BF16)
    got = other_core(theirs)
    send = (mine[1:] + got[1:].astype(F32)).astype(BF16)
    summed = mine[0] + got[0].astype(F32)
    for k in range(1, n_x):
        summed = summed + from_x(send[k - 1], n_x - k).astype(F32)
    for c in range(1, chunks - 1):
        grads = weights(c, after(rows, send), grads)
    summed = after(summed, grads[0])
    rounded = summed.astype(BF16)
    if chunks > 1:
        grads = weights(chunks - 1, after(rows, rounded), grads)

    def for_blk(array, step):
        return lax.dynamic_index_in_dim(array, lax.rem(own + step, n_blk), 0, keepdims=False)

    pieces = [
        lax.ppermute(for_blk(rounded, k), "blk", [(i, (i + k) % n_blk) for i in range(n_blk)])
        for k in range(1, n_blk)
    ]
    input_grad = for_blk(summed, 0)
    for piece in pieces:
        input_grad = input_grad + piece.astype(F32)

    return input_grad.astype(BF16), *grads


def solution(mesh):
    in_specs = (
        P(("group", "dp"), "blk"),
        P(("group", "dp"), "blk"),
        P("dp", "blk", None, None),
        P("dp", "blk", None, None),
        P("dp", "blk", None, None),
        P(),
        P(),
        P(),
        P(),
    )
    out_specs = (
        P(("group", "dp"), "blk"),
        P("dp", ("group", "blk"), None, None),
        P("dp", ("group", "blk"), None, None),
        P("dp", ("group", "blk"), None, None),
    )
    return jax.shard_map(body, mesh=mesh, in_specs=in_specs, out_specs=out_specs, check_vma=False)
```
